32 devices in a mesh: dp: 8 (over z, y), tensor: 4 (over x, core).
Axes of the slice: x: 2, y: 2, z: 4, core: 2. Of those that a mesh axis runs over, the one named last changes fastest.
Arguments:
- residual: bfloat16 [4096, 2048], P(('dp', 'tensor')), may hold values from -0.59765625 to 0.59765625
- queries: bfloat16 [4096, 2048], P(('dp', 'tensor')), may hold values from -27 to 27
- new_keys: bfloat16 [4096, 2048], P(('dp', 'tensor')), may hold values from -27 to 27
- new_values: bfloat16 [4096, 2048], P(('dp', 'tensor')), may hold values from -6 to 6
- lengths: int32 [8, 2], P('dp'), may hold values from 1 to 384, 512 in all within a row
- page_order: int32 [8, 5], P('dp'), may hold values from 0 to 4, each once within a row
- wo_shard: float32 [2048, 2048], P('tensor', 'dp'), may hold values from -0.125 to 0.125
- norm_gain: float32 [2048], replicated, may hold values from 0.1 to 1.9
- gate_shard: float32 [4, 2048, 256], P('tensor', 'dp'), may hold values from -0.125 to 0.125
- up_shard: float32 [4, 2048, 256], P('tensor', 'dp'), may hold values from -0.125 to 0.125
- down_shard: float32 [4, 256, 2048], P('tensor', None, 'dp'), may hold values from -0.1875 to 0.1875
- routes: int32 [4096, 8], P(('dp', 'tensor')), may hold values from 0 to 63, as said below
- route_weights: float32 [4096, 8], P(('dp', 'tensor')), may hold values from 0.05 to 0.3
Outputs:
- hidden_mid: bfloat16 [4096, 2048], P(('dp', 'tensor'))
- expert_sum: bfloat16 [4096, 2048], P(('dp', 'tensor'))
- key_pages: bfloat16 [40, 128, 2048], P('dp', None, 'tensor')
- value_pages: bfloat16 [40, 128, 2048], P('dp', None, 'tensor')
The draws below stay inside these ranges and needn't reach their ends.
Inputs may be any that keep to these rules, and one draw needn't show every extreme that they name: `routes`: each row names 8 different experts. Within each aligned block of 128 rows (the rows of one device), each expert below 1 is named by 1 to 16 rows; one of them, the same in all blocks of a draw, by exactly 16 rows in every block, the others by at most 8 rows.
All inputs are finite; a program needn't handle non-finite values.
Results may differ from the reference program's by a relative error of at most 0.015.
Values may be sent and summed in bfloat16 or wider, within the bound.
A program may use at most 64 MiB of HBM per device.

```python
import math
import jax
import jax.numpy as jnp
import numpy as np
from jax import lax

D = 2048
HEADS = 16
HD = 128
FF = 1024
EXPERTS = 64
TOP = 8
SPLIT = 4
PAGE = 128
REQ_GRP = 2
TOK_DEV = 128
ATT = 2048
PIECE = 256
FLIGHT = 1
TOK_GRP = 512
TOKENS = 4096
POOL = 5
MOST = 16
N_DP = 8
N_TENSOR = 4


def pair_draw(key):
    base_query = jax.random.normal(jax.random.fold_in(key, 11), (TOKENS, ATT), jnp.float32)
    base_key = jax.random.normal(jax.random.fold_in(key, 12), (TOKENS, ATT), jnp.float32)
    queries_out = 1.5 * jnp.clip(base_query, -6.0, 6.0)
    keys_out = jnp.clip(base_key, -6.0, 6.0)
    return (queries_out, keys_out)


def draw_queries(key, part):
    return pair_draw(key)[0].astype(jnp.bfloat16)


def draw_new_keys(key, part):
    return pair_draw(key)[1].astype(jnp.bfloat16)


def draw_routes(key, part):
    blocks = TOKENS // TOK_DEV
    flight = N_TENSOR // SPLIT
    hottest = jax.random.randint(jax.random.fold_in(key, 21), (), 0, flight)
    counts = jax.random.randint(jax.random.fold_in(key, 22), (blocks, flight), 1, MOST // 2 + 1)
    counts = jnp.where(jnp.arange(flight)[None, :] == hottest, MOST, counts)

    def permute_rows(subkey):
        return jax.random.permutation(subkey, TOK_DEV)
    orders = jax.vmap(permute_rows)(jax.random.split(jax.random.fold_in(key, 23), blocks * flight))
    rank_of = jnp.argsort(orders.reshape(blocks, flight, TOK_DEV), axis=2)
    chosen = rank_of < counts[:, :, None]
    chosen = jnp.transpose(chosen, (0, 2, 1)).reshape(TOKENS, flight)

    def permute_rest(subkey):
        return jax.random.permutation(subkey, EXPERTS - flight)
    others = jax.vmap(permute_rest)(jax.random.split(jax.random.fold_in(key, 24), TOKENS)) + flight
    in_ids = jnp.broadcast_to(jnp.arange(flight)[None, :], (TOKENS, flight))
    all_ids = jnp.concatenate([in_ids, others], axis=1)
    score_in = jnp.where(chosen, in_ids, EXPERTS + in_ids)
    score_rest = jnp.broadcast_to(flight + jnp.arange(EXPERTS - flight)[None, :], (TOKENS, EXPERTS - flight))
    scores = jnp.concatenate([score_in, score_rest], axis=1)
    position = jnp.argsort(scores, axis=1)[:, :TOP]
    picked = jnp.take_along_axis(all_ids, position, axis=1)

    def permute_slots(subkey):
        return jax.random.permutation(subkey, TOP)
    shuffle = jax.vmap(permute_slots)(jax.random.split(jax.random.fold_in(key, 25), TOKENS))
    return jnp.take_along_axis(picked, shuffle, axis=1).astype(jnp.int32)


def levels(rng, extent, cuts, low, top_value):
    factor_of, own = 1.0, jax.random.fold_in(rng, 6)
    for axis_at, parts in cuts:
        steps = jnp.exp(jax.random.uniform(jax.random.fold_in(own, axis_at), (parts,), jnp.float32, low / len(cuts), top_value / len(cuts)))
        factor_of = factor_of * jnp.repeat(steps, extent[axis_at] // parts).reshape([-1 if axis == axis_at else 1 for axis in range(len(extent))])
    return factor_of


def profile(amount, total, most, skew):
    portions = [(1 << 20) // math.isqrt(rank ** skew) + 1 for rank in range(2, amount + 1)]
    surplus, given = total - most - (amount - 1), [1] * (amount - 1)
    while surplus > 0:
        candidates = [i for i in range(amount - 1) if given[i] < most]
        mass, remaining = sum([portions[i] for i in candidates]), surplus
        for i in candidates:
            addition = min(most - given[i], max(1, remaining * portions[i] // mass), surplus)
            given[i] = given[i] + addition
            surplus = surplus - addition
    return np.array([most] + given)


def ragged_sizes(rng, number_of, total, reach, lean):
    if number_of == 2:
        one = jax.random.randint(rng, (), max(1, total - reach), min(reach, total - 1) + 1)
        return jnp.stack([one, total - one])
    tallies = jnp.asarray(profile(number_of, total, reach, lean), jnp.int32)
    couples = (number_of - 1) // 2
    donor, receiver = tallies[1:1 + 2 * couples:2], tallies[2:2 + 2 * couples:2]
    slack = jnp.minimum(donor - 1, reach - receiver)
    moved = jax.random.randint(jax.random.fold_in(rng, 1), (couples,), 0, 1 << 20) % (slack + 1)
    tallies = tallies.at[1:1 + 2 * couples:2].set(donor - moved).at[2:2 + 2 * couples:2].set(receiver + moved)
    return tallies[jax.random.permutation(jax.random.fold_in(rng, 2), number_of)]


def gaussian(stream_key, shape, width, most, shards=(), held_as=jnp.bfloat16):
    entries = width * jax.random.normal(stream_key, shape, jnp.float32)
    if shards:
        entries = entries * levels(stream_key, shape, shards, -0.22, 0.18)
    return jnp.clip(entries, -most, most).astype(held_as)


def setup_inputs(seed: int = 0) -> dict:
    keys = jax.random.split(jax.random.key(seed), 14)
    residual = gaussian(keys[0], (TOKENS, D), 0.1, 0.59765625, ((0, 32),))
    queries = draw_queries(jax.random.fold_in(keys[13], 71), 0)
    new_keys = draw_new_keys(jax.random.fold_in(keys[13], 71), 0)
    new_values = gaussian(keys[3], (TOKENS, ATT), 1.0, 6.0, ((0, 32),))
    lengths = jax.vmap(lambda own: ragged_sizes(own, REQ_GRP, TOK_GRP, TOK_GRP * 3 // 4, 2))(jax.random.split(keys[4], N_DP)).reshape((N_DP, REQ_GRP)).astype(jnp.int32)
    page_order = jax.vmap(lambda own: jax.random.permutation(own, POOL))(jax.random.split(keys[5], N_DP)).reshape((N_DP, POOL)).astype(jnp.int32)
    wo_shard = gaussian(keys[6], (ATT, D), ATT ** -0.5, 0.125, ((0, 4), (1, 8)), jnp.float32)
    norm_gain = jnp.clip(1.0 + 0.18 * jax.random.normal(keys[7], (D,), jnp.float32), 0.1, 1.9)
    gate_shard = gaussian(keys[8], (N_TENSOR, D, PIECE), D ** -0.5, 0.125, ((0, 4), (1, 8)), jnp.float32)
    up_shard = gaussian(keys[9], (N_TENSOR, D, PIECE), D ** -0.5, 0.125, ((0, 4), (1, 8)), jnp.float32)
    down_shard = gaussian(keys[10], (N_TENSOR, PIECE, D), FF ** -0.5, 0.1875, ((0, 4), (2, 8)), jnp.float32)
    routes = draw_routes(jax.random.fold_in(keys[13], 71), 0)
    route_weights = jnp.clip(0.05 + 0.25 * jax.random.uniform(keys[12], (TOKENS, TOP), jnp.float32) ** levels(keys[12], (TOKENS, TOP), ((0, 32),), -0.2, 0.2), 0.05, 0.3)
    return {"residual": residual, "queries": queries, "new_keys": new_keys, "new_values": new_values, "lengths": lengths, "page_order": page_order, "wo_shard": wo_shard, "norm_gain": norm_gain, "gate_shard": gate_shard, "up_shard": up_shard, "down_shard": down_shard, "routes": routes, "route_weights": route_weights}


def page_layout(lens_row, order_row, group_rows, pool_size):
    index_rows = jnp.arange(group_rows, dtype=jnp.int32)
    prompt_ends = jnp.cumsum(lens_row).astype(jnp.int32)
    segment = lax.optimization_barrier(jnp.sum((index_rows[:, None] >= prompt_ends[None, :]).astype(jnp.int32), axis=1))
    prompt_starts = prompt_ends - lens_row
    owner_mask = (segment[:, None] == jnp.arange(lens_row.shape[0], dtype=jnp.int32)[None, :]).astype(jnp.int32)
    begins = lax.optimization_barrier(jnp.sum(owner_mask * prompt_starts[None, :], axis=1))
    page_count = (lens_row + PAGE - 1) // PAGE
    first_page = jnp.cumsum(page_count).astype(jnp.int32) - page_count
    page_first = lax.optimization_barrier(jnp.sum(owner_mask * first_page[None, :], axis=1))
    position = index_rows - begins
    logical = page_first + position // PAGE
    matched = (logical[:, None] == jnp.arange(pool_size, dtype=jnp.int32)[None, :]).astype(jnp.int32)
    physical = lax.optimization_barrier(jnp.sum(matched * order_row[None, :], axis=1))
    return (segment, physical * PAGE + position % PAGE)

def attend_group(q_group, k_group, v_group, segment):
    block_rows = min(512, TOK_GRP)
    count_blocks = TOK_GRP // block_rows
    q_blocks = q_group.reshape(count_blocks, block_rows, HEADS, HD)
    seg_blocks = segment.reshape(count_blocks, block_rows)
    k_float = k_group.reshape(TOK_GRP, HEADS, HD).astype(jnp.float32)
    v_float = v_group.reshape(TOK_GRP, HEADS, HD).astype(jnp.float32)

    def one_block(block_pair):
        q_block, seg_block = block_pair
        scores = jnp.einsum('qhd,khd->hqk', q_block.astype(jnp.float32), k_float) / math.sqrt(HD)
        same_prompt = seg_block[:, None] == segment[None, :]
        scores = jnp.where(same_prompt[None, :, :], scores, -jnp.inf)
        row_max = lax.optimization_barrier(jnp.max(scores, axis=2, keepdims=True))
        weights = jnp.exp(scores - row_max)
        totals = lax.optimization_barrier(jnp.sum(weights, axis=2))
        rounded = lax.optimization_barrier(weights.astype(jnp.bfloat16)).astype(jnp.float32)
        output = jnp.einsum('hqk,khd->qhd', rounded, v_float) / jnp.transpose(totals)[:, :, None]
        return output.astype(jnp.bfloat16).reshape(block_rows, HEADS * HD)
    return lax.map(one_block, (q_blocks, seg_blocks)).reshape(TOK_GRP, HEADS * HD)

def reference(residual, queries, new_keys, new_values, lengths, page_order, wo_shard, norm_gain, gate_shard, up_shard, down_shard, routes, route_weights):

    def per_group(group):
        first_row = (group * TOK_GRP).astype(jnp.int32)
        q_group = lax.dynamic_slice_in_dim(queries, first_row, TOK_GRP, 0)
        k_group = lax.dynamic_slice_in_dim(new_keys, first_row, TOK_GRP, 0)
        v_group = lax.dynamic_slice_in_dim(new_values, first_row, TOK_GRP, 0)
        segment, slot_index = page_layout(lengths[group], page_order[group], TOK_GRP, POOL)
        attended = attend_group(q_group, k_group, v_group, segment)
        key_block = jnp.zeros((POOL * PAGE, ATT), jnp.bfloat16).at[slot_index].set(k_group)
        value_block = jnp.zeros((POOL * PAGE, ATT), jnp.bfloat16).at[slot_index].set(v_group)
        return (attended, key_block, value_block)
    attended, key_block, value_block = lax.map(per_group, jnp.arange(N_DP, dtype=jnp.int32))
    attended = attended.reshape(TOKENS, ATT)
    key_pages = key_block.reshape(N_DP * POOL, PAGE, ATT)
    value_pages = value_block.reshape(N_DP * POOL, PAGE, ATT)
    wo_cast = wo_shard.astype(jnp.bfloat16)
    projected = jnp.dot(attended, wo_cast, preferred_element_type=jnp.float32)
    hidden_mid = (residual.astype(jnp.float32) + projected).astype(jnp.bfloat16)
    mid_float = hidden_mid.astype(jnp.float32)
    normed = (mid_float * lax.rsqrt(lax.optimization_barrier(jnp.mean(mid_float * mid_float, axis=1, keepdims=True)) + 1e-06) * norm_gain).astype(jnp.bfloat16)
    blocks = TOKENS // TOK_DEV
    normed_blocks = normed.reshape(blocks, TOK_DEV, D).astype(jnp.float32)
    route_blocks = routes.reshape(blocks, TOK_DEV, TOP)
    weight_blocks = route_weights.reshape(blocks, TOK_DEV, TOP)
    flight_ids = jnp.arange(FLIGHT, dtype=jnp.int32)
    named_here = route_blocks[:, :, :, None] == flight_ids[None, None, None, :]
    routed = jnp.any(named_here, axis=2)
    weight_sum = lax.optimization_barrier(jnp.sum(jnp.where(named_here, weight_blocks[:, :, :, None], 0.0), axis=2))
    ranked = jnp.cumsum(routed.astype(jnp.int32), axis=1) - 1
    picked = ((ranked[:, :, :, None] == jnp.arange(MOST, dtype=jnp.int32)[None, None, None, :]) & routed[:, :, :, None]).astype(jnp.float32)
    mixing = picked * weight_sum[:, :, :, None]

    def per_expert(expert, running):
        chosen = lax.dynamic_index_in_dim(picked, expert, 2, keepdims=False)
        gathered = jnp.einsum('btm,btd->bmd', chosen, normed_blocks, precision=lax.Precision.HIGHEST)
        expert_rows = gathered.astype(jnp.bfloat16).reshape(blocks * MOST, D)
        summed = jnp.zeros((blocks * MOST, D), jnp.float32)
        for part_index in range(SPLIT):
            piece_index = (expert * SPLIT + part_index).astype(jnp.int32)
            gate_w = lax.dynamic_index_in_dim(gate_shard, piece_index, 0, keepdims=False).astype(jnp.bfloat16)
            up_w = lax.dynamic_index_in_dim(up_shard, piece_index, 0, keepdims=False).astype(jnp.bfloat16)
            down_w = lax.dynamic_index_in_dim(down_shard, piece_index, 0, keepdims=False).astype(jnp.bfloat16)
            gate_val = jnp.dot(expert_rows, gate_w, preferred_element_type=jnp.float32)
            up_val = jnp.dot(expert_rows, up_w, preferred_element_type=jnp.float32)
            inner_act = (jax.nn.silu(gate_val) * up_val).astype(jnp.bfloat16)
            result = jnp.dot(inner_act, down_w, preferred_element_type=jnp.float32).astype(jnp.bfloat16)
            summed = summed + result.astype(jnp.float32)
        weighting = lax.dynamic_index_in_dim(mixing, expert, 2, keepdims=False)
        added = jnp.einsum('btm,bmd->btd', weighting, summed.reshape(blocks, MOST, D), precision=lax.Precision.HIGHEST)
        return running + added
    total_sum = lax.fori_loop(0, FLIGHT, per_expert, jnp.zeros((blocks, TOK_DEV, D), jnp.float32))
    expert_sum = total_sum.reshape(TOKENS, D).astype(jnp.bfloat16)
    return (hidden_mid, expert_sum, key_pages, value_pages)
```

```python
import math

import jax
import jax.numpy as jnp
from jax import lax
from jax.sharding import PartitionSpec as P

D = 2048
HEADS = 16
HD = 128
SPLIT = 4
PAGE = 128
MOST = 16


def running(values):
    ids = jnp.arange(values.shape[0], dtype=jnp.int32)
    return jnp.sum(jnp.where(ids[:, None] >= ids[None, :], values[None, :], 0), axis=1)


def page_layout(lens_row, order_row, group_rows, pool_size):
    index_rows = jnp.arange(group_rows, dtype=jnp.int32)
    prompt_ends = running(lens_row)
    segment = jnp.sum((index_rows[:, None] >= prompt_ends[None, :]).astype(jnp.int32), axis=1)
    prompt_starts = prompt_ends - lens_row
    owner_mask = (
        segment[:, None] == jnp.arange(lens_row.shape[0], dtype=jnp.int32)[None, :]
    ).astype(jnp.int32)
    begins = jnp.sum(owner_mask * prompt_starts[None, :], axis=1)
    page_count = (lens_row + PAGE - 1) // PAGE
    first_page = running(page_count) - page_count
    page_first = jnp.sum(owner_mask * first_page[None, :], axis=1)
    position = index_rows - begins
    logical = page_first + position // PAGE
    matched = (logical[:, None] == jnp.arange(pool_size, dtype=jnp.int32)[None, :]).astype(
        jnp.int32
    )
    physical = jnp.sum(matched * order_row[None, :], axis=1)
    return (segment, physical * PAGE + position % PAGE)


def attend_group(q_heads, k_heads, v_heads, segment, heads_here):
    group_rows = q_heads.shape[0]
    block_rows = min(512, group_rows)
    count_blocks = group_rows // block_rows
    q_blocks = q_heads.reshape(count_blocks, block_rows, heads_here, HD)
    seg_blocks = segment.reshape(count_blocks, block_rows)
    k_split = k_heads.reshape(group_rows, heads_here, HD)
    v_split = v_heads.reshape(group_rows, heads_here, HD)

    def one_block(block_pair):
        q_block, seg_block = block_pair
        scores = jnp.einsum(
            "qhd,khd->hqk", q_block, k_split, preferred_element_type=jnp.float32
        ) / math.sqrt(HD)
        same_prompt = seg_block[:, None] == segment[None, :]
        scores = jnp.where(same_prompt[None, :, :], scores, -jnp.inf)
        row_max = jnp.max(scores, axis=2, keepdims=True)
        weights = jnp.exp(scores - row_max)
        totals = jnp.sum(weights, axis=2)
        output = jnp.einsum(
            "hqk,khd->qhd",
            weights.astype(jnp.bfloat16),
            v_split,
            preferred_element_type=jnp.float32,
        )
        output = output / jnp.transpose(totals)[:, :, None]
        return output.astype(jnp.bfloat16).reshape(block_rows, heads_here * HD)

    return lax.map(one_block, (q_blocks, seg_blocks)).reshape(group_rows, heads_here * HD)


def body(
    residual,
    queries,
    new_keys,
    new_values,
    lengths,
    page_order,
    wo_shard,
    norm_gain,
    gate_shard,
    up_shard,
    down_shard,
    routes,
    route_weights,
):
    tensor_count = lax.axis_size("tensor")
    heads_here = HEADS // tensor_count
    q_heads, k_heads, v_heads = (
        lax.all_to_all(queries, "tensor", split_axis=1, concat_axis=0, tiled=True),
        lax.all_to_all(new_keys, "tensor", split_axis=1, concat_axis=0, tiled=True),
        lax.all_to_all(new_values, "tensor", split_axis=1, concat_axis=0, tiled=True),
    )
    group_rows = q_heads.shape[0]
    pool_size = page_order.shape[1]
    segment, slot_index = page_layout(lengths[0], page_order[0], group_rows, pool_size)
    head_width = k_heads.shape[1]
    key_pages = (
        jnp.zeros((pool_size * PAGE, head_width), jnp.bfloat16)
        .at[slot_index]
        .set(k_heads)
        .reshape(pool_size, PAGE, head_width)
    )
    value_pages = (
        jnp.zeros((pool_size * PAGE, head_width), jnp.bfloat16)
        .at[slot_index]
        .set(v_heads)
        .reshape(pool_size, PAGE, head_width)
    )
    attended = attend_group(q_heads, k_heads, v_heads, segment, heads_here)
    columns = lax.all_gather(wo_shard.astype(jnp.bfloat16), "dp", axis=1, tiled=True)
    partial = jnp.dot(attended, columns, preferred_element_type=jnp.float32).astype(jnp.bfloat16)
    tokens_here = residual.shape[0]
    parts = lax.all_to_all(partial, "tensor", split_axis=0, concat_axis=0, tiled=True)
    projected = jnp.sum(
        parts.reshape(tensor_count, tokens_here, D).astype(jnp.float32), axis=0
    )
    hidden_mid = (residual.astype(jnp.float32) + projected).astype(jnp.bfloat16)
    mid_float = hidden_mid.astype(jnp.float32)
    normed = (
        mid_float
        * lax.rsqrt(jnp.mean(mid_float * mid_float, axis=1, keepdims=True) + 1e-06)
        * norm_gain
    ).astype(jnp.bfloat16)
    flight = tensor_count // SPLIT
    flight_ids = jnp.arange(flight, dtype=jnp.int32)
    named_here = routes[:, :, None] == flight_ids[None, None, :]
    routed = jnp.any(named_here, axis=1)
    weight_sum = jnp.sum(jnp.where(named_here, route_weights[:, :, None], 0.0), axis=1)
    row_ids = jnp.arange(routed.shape[0], dtype=jnp.int32)
    lower = (row_ids[:, None] >= row_ids[None, :]).astype(jnp.bfloat16)
    ranked = (
        jnp.dot(lower, routed.astype(jnp.bfloat16), preferred_element_type=jnp.float32).astype(jnp.int32) - 1
    )
    picked = (ranked[:, :, None] == jnp.arange(MOST, dtype=jnp.int32)[None, None, :]) & routed[
        :, :, None
    ]
    outgoing = jnp.einsum(
        "tem,td->emd", picked.astype(jnp.bfloat16), normed, preferred_element_type=jnp.float32
    ).astype(jnp.bfloat16)
    outgoing = jnp.repeat(outgoing, SPLIT, axis=0)
    gate_full, up_full, down_full = (
        lax.all_gather(gate_shard.astype(jnp.bfloat16), "dp", axis=1, tiled=True),
        lax.all_gather(up_shard.astype(jnp.bfloat16), "dp", axis=1, tiled=True),
        lax.all_gather(down_shard.astype(jnp.bfloat16), "dp", axis=2, tiled=True),
    )
    arrived = lax.all_to_all(outgoing, "tensor", split_axis=0, concat_axis=0, tiled=True)
    gate_val = jnp.einsum("smd,dp->smp", arrived, gate_full[0], preferred_element_type=jnp.float32)
    up_val = jnp.einsum("smd,dp->smp", arrived, up_full[0], preferred_element_type=jnp.float32)
    inner_act = (jax.nn.silu(gate_val) * up_val).astype(jnp.bfloat16)
    result = jnp.einsum(
        "smp,pd->smd", inner_act, down_full[0], preferred_element_type=jnp.float32
    ).astype(jnp.bfloat16)
    returned = lax.all_to_all(result, "tensor", split_axis=0, concat_axis=0, tiled=True)
    summed = jnp.sum(returned.reshape(flight, SPLIT, MOST, D).astype(jnp.float32), axis=1)
    mixing = picked.astype(jnp.float32) * weight_sum[:, :, None]
    expert_sum = jnp.einsum("tem,emd->td", mixing, summed, precision=lax.Precision.HIGHEST).astype(
        jnp.bfloat16
    )
    return (hidden_mid, expert_sum, key_pages, value_pages)


def solution(mesh):
    return jax.shard_map(
        body,
        mesh=mesh,
        in_specs=(
            P(("dp", "tensor"), None),
            P(("dp", "tensor"), None),
            P(("dp", "tensor"), None),
            P(("dp", "tensor"), None),
            P("dp", None),
            P("dp", None),
            P("tensor", "dp"),
            P(),
            P("tensor", "dp", None),
            P("tensor", "dp", None),
            P("tensor", None, "dp"),
            P(("dp", "tensor"), None),
            P(("dp", "tensor"), None),
        ),
        out_specs=(
            P(("dp", "tensor"), None),
            P(("dp", "tensor"), None),
            P("dp", None, "tensor"),
            P("dp", None, "tensor"),
        ),
        check_vma=False,
    )
```

```python
import functools
import math

import jax
import jax.numpy as jnp
from jax import lax
from jax.experimental import pallas as pl
from jax.experimental.pallas import tpu as pltpu
from jax.sharding import PartitionSpec as P

HEADS = 16
HD = 128
SPLIT = 4
PAGE = 128
MOST = 16
MESH = pl.DeviceIdType.MESH
BF = jnp.bfloat16
F32 = jnp.float32


def dot(a, b):
    return jnp.dot(a, b, preferred_element_type=F32)


class Stream:
    def __init__(self, buf, sems, dp_at, place, lines, pair_stride, line_stride, me_t):
        self.buf, self.sems, self.lines, self.me_t = buf, sems, lines, me_t
        self.pos, self.side = place
        self.pair_stride, self.line_stride = pair_stride, line_stride

    def shard(self, pos, side):
        return pos * self.line_stride + side * self.pair_stride

    def copy(self, kind, k, d, target):
        block = self.buf.at[d]
        return pltpu.make_async_remote_copy(
            src_ref=block,
            dst_ref=block,
            send_sem=self.sems.at[kind, 0, k],
            recv_sem=self.sems.at[kind, 1, k],
            device_id=(target, self.me_t),
            device_id_type=MESH,
        )

    def up(self, k):
        return self.copy(0, k, self.shard(self.pos - k, self.side), self.shard(self.pos + 1, self.side))

    def down(self, k):
        return self.copy(1, k, self.shard(self.pos + k, self.side), self.shard(self.pos - 1, self.side))

    def across(self, q):
        return self.copy(2, q, self.shard(q, self.side), self.shard(self.pos, 1 - self.side))

    def start(self):
        pos, last = self.pos, self.lines - 1

        @pl.when(pos < last)
        def _():
            self.up(0).start()

        @pl.when(pos > 0)
        def _():
            self.down(0).start()

        self.across(pos).start()

    def step(self, k):
        pos, last = self.pos, self.lines - 1

        @pl.when(pos - 1 - k >= 0)
        def _():
            d = self.shard(pos - 1 - k, self.side)
            self.copy(0, k, d, self.shard(pos, self.side)).wait_recv()
            if k + 1 <= last - 1:

                @pl.when(pos < last)
                def _():
                    self.up(k + 1).start()

            self.across(pos - 1 - k).start()

        @pl.when(pos + 1 + k <= last)
        def _():
            d = self.shard(pos + 1 + k, self.side)
            self.copy(1, k, d, self.shard(pos, self.side)).wait_recv()
            if k + 1 <= last - 1:

                @pl.when(pos > 0)
                def _():
                    self.down(k + 1).start()

            self.across(pos + 1 + k).start()

    def arrived(self):
        for q in range(self.lines):
            d = self.shard(q, 1 - self.side)
            self.copy(2, q, d, self.shard(self.pos, 1 - self.side)).wait_recv()

    def sent(self):
        pos, last = self.pos, self.lines - 1
        for k in range(last):

            @pl.when((pos - k >= 0) & (pos < last))
            def _():
                self.up(k).wait_send()

            @pl.when((pos + k <= last) & (pos > 0))
            def _():
                self.down(k).wait_send()

        for q in range(self.lines):
            self.across(q).wait_send()


def layer_kernel(
    dims,
    lengths,
    order,
    q_in,
    k_in,
    v_in,
    residual,
    wo,
    gain,
    gate,
    up,
    down,
    routes,
    route_weights,
    hidden_out,
    expert_out,
    key_out,
    value_out,
    wo_all,
    gu_all,
    down_all,
    q_all,
    k_all,
    v_all,
    attended,
    part,
    recv_pair,
    send_x,
    recv_x,
    total,
    rows_out,
    rows_in,
    piece_out,
    piece_in,
    weight_sems,
    qkv_sems,
    own_sems,
    pair_sems,
    x_sems,
    row_sems,
    piece_sems,
):
    dp, tensor, pair_stride, line_stride = dims
    lines = dp // 2
    toks, width = q_in.shape
    head_width = width // tensor
    heads = head_width // HD
    group = toks * tensor
    columns = wo.shape[1]
    flight = tensor // SPLIT
    xs = tensor // 2
    me_d, me_t = lax.axis_index("dp"), lax.axis_index("tensor")
    me_x, me_c = lax.div(me_t, 2), lax.rem(me_t, 2)
    if pair_stride == 1:
        pos, side = lax.div(me_d, 2), lax.rem(me_d, 2)
    else:
        pos, side = lax.rem(me_d, lines), lax.div(me_d, lines)
    place = (pos, side)
    streams = [
        Stream(buf, weight_sems.at[i], me_d, place, lines, pair_stride, line_stride, me_t)
        for i, buf in enumerate((wo_all, gu_all, down_all))
    ]
    wo_s, gu_s, down_s = streams
    peers = [lax.rem(me_t + i, tensor) for i in range(tensor)]
    sources = [lax.rem(me_t + tensor - i, tensor) for i in range(tensor)]

    barrier = pltpu.get_barrier_semaphore()
    for i in range(1, tensor):
        pl.semaphore_signal(barrier, inc=1, device_id=(me_d, peers[i]), device_id_type=MESH)
    pl.semaphore_signal(
        barrier, inc=1, device_id=(wo_s.shard(pos, 1 - side), me_t), device_id_type=MESH
    )

    @pl.when(pos < lines - 1)
    def _():
        pl.semaphore_signal(
            barrier, inc=1, device_id=(wo_s.shard(pos + 1, side), me_t), device_id_type=MESH
        )

    @pl.when(pos > 0)
    def _():
        pl.semaphore_signal(
            barrier, inc=1, device_id=(wo_s.shard(pos - 1, side), me_t), device_id_type=MESH
        )

    wo_all[me_d] = wo[...].astype(BF)
    neighbours = (pos < lines - 1).astype(jnp.int32) + (pos > 0).astype(jnp.int32)
    pl.semaphore_wait(barrier, tensor + neighbours)

    wo_s.start()

    mine = pl.ds(pl.multiple_of(me_t * toks, toks), toks)

    def head_cols(t):
        return pl.ds(pl.multiple_of(t * head_width, head_width), head_width)

    triples = ((q_in, q_all), (k_in, k_all), (v_in, v_all))

    def qkv_copy(n, i):
        src, dst = triples[n]
        return pltpu.make_async_remote_copy(
            src_ref=src.at[:, head_cols(peers[i])],
            dst_ref=dst.at[mine, :],
            send_sem=qkv_sems.at[n, 0, i],
            recv_sem=qkv_sems.at[n, 1, i],
            device_id=(me_d, peers[i]),
            device_id_type=MESH,
        )

    def own_copy(n):
        src, dst = triples[n]
        return pltpu.make_async_copy(src.at[:, head_cols(me_t)], dst.at[mine, :], own_sems.at[n])

    for n in range(3):
        for i in range(1, tensor):
            qkv_copy(n, i).start()
        own_copy(n).start()

    gu_all[me_d, 0] = gate[0].astype(BF)
    gu_all[me_d, 1] = up[0].astype(BF)
    gu_s.start()
    down_all[me_d] = down[0].astype(BF)
    down_s.start()

    prompts, pool = lengths.shape[1], order.shape[1]
    starts, ends, firsts = [], [], []
    begin, page = 0, 0
    for r in range(prompts):
        starts.append(begin)
        firsts.append(page)
        begin = begin + lengths[0, r]
        page = page + ((lengths[0, r] + (PAGE - 1)) >> 7)
        ends.append(begin)

    def segment_of(index):
        return sum((index >= end).astype(jnp.int32) for end in ends)

    row_index = lax.broadcasted_iota(jnp.int32, (1, group), 1)
    seg_row = segment_of(row_index)
    slot = jnp.zeros((1, group), jnp.int32)
    for r in range(prompts):
        position = row_index - starts[r]
        logical = firsts[r] + (position >> 7)
        physical = jnp.zeros((1, group), jnp.int32)
        for p in range(pool):
            physical = physical + jnp.where(logical == p, order[0, p], 0)
        slot = jnp.where(seg_row == r, physical * PAGE + (position & (PAGE - 1)), slot)

    def source_rows(i):
        return pl.ds(pl.multiple_of(sources[i] * toks, toks), toks)

    def qkv_arrived(n):
        src, dst = triples[n]
        for i in range(1, tensor):
            pltpu.make_async_remote_copy(
                src_ref=src.at[:, head_cols(me_t)],
                dst_ref=dst.at[source_rows(i), :],
                send_sem=qkv_sems.at[n, 0, i],
                recv_sem=qkv_sems.at[n, 1, i],
                device_id=(me_d, sources[i]),
                device_id_type=MESH,
            ).wait_recv()
        own_copy(n).wait()

    q_rows = min(512, group)

    def attend(h):
        cols = slice(h * HD, (h + 1) * HD)

        def block(first):
            q = q_all[pl.ds(first, q_rows), cols]
            scores = lax.dot_general(
                q, k_all[:, cols], (((1,), (1,)), ((), ())), preferred_element_type=F32
            ) * (1.0 / math.sqrt(HD))
            index = lax.broadcasted_iota(jnp.int32, (q_rows, 1), 0) + first
            scores = jnp.where(segment_of(index) == seg_row, scores, -jnp.inf)
            weights = jnp.exp(scores - jnp.max(scores, axis=1, keepdims=True))
            sums = jnp.sum(weights, axis=1, keepdims=True)
            out = dot(weights.astype(BF), v_all[:, cols]) / sums
            attended[pl.ds(first, q_rows), cols] = out.astype(BF)

        if group == q_rows:
            block(0)
        else:

            @pl.loop(0, group // q_rows)
            def _(b):
                block(pl.multiple_of(b * q_rows, q_rows))

    def write_pages(values, out):
        @pl.loop(0, pool)
        def _(p):
            wanted = lax.broadcasted_iota(jnp.int32, (PAGE, group), 0) + p * PAGE
            hit = jnp.where(wanted == slot, 1.0, 0.0).astype(BF)
            out[p] = dot(hit, values[...]).astype(BF)

    wo_s.step(0)
    gu_s.step(0)
    qkv_arrived(0)
    qkv_arrived(1)
    down_s.step(0)
    qkv_arrived(2)
    for h in range(heads):
        attend(h)
        if h == heads // 2:
            wo_s.step(1)
    gu_s.step(1)
    write_pages(k_all, key_out)
    down_s.step(1)
    for k in range(2, lines - 1):
        wo_s.step(k)
        gu_s.step(k)
    write_pages(v_all, value_out)

    ids = lax.broadcasted_iota(jnp.int32, (toks, toks), 0)
    lanes = lax.broadcasted_iota(jnp.int32, (toks, toks), 1)
    lower = jnp.where(ids >= lanes, 1.0, 0.0).astype(BF)
    picks, mixes = [], []
    for e in range(flight):
        named = routes[...] == e
        routed = jnp.max(jnp.where(named, 1.0, 0.0), axis=1, keepdims=True)
        mixes.append(jnp.sum(jnp.where(named, route_weights[...], 0.0), axis=1, keepdims=True))
        spread = jnp.broadcast_to(routed, (toks, toks))
        rank = dot(lower, spread.astype(BF)).astype(jnp.int32) - 1
        picks.append(jnp.where((rank == lanes) & (spread > 0.5), 1.0, 0.0))

    chunks = 4
    chunk = width // chunks
    per_chunk = dp // chunks
    partner = (me_d, me_t + 1 - 2 * me_c)

    def pair_copy(j):
        cols = pl.ds(j * chunk, chunk)
        return pltpu.make_async_remote_copy(
            src_ref=part.at[1 - me_c, :, :, cols],
            dst_ref=recv_pair.at[:, :, cols],
            send_sem=pair_sems.at[0, j],
            recv_sem=pair_sems.at[1, j],
            device_id=partner,
            device_id_type=MESH,
        )

    def x_copy(i, j):
        cols = pl.ds(j * chunk, chunk)
        return pltpu.make_async_remote_copy(
            src_ref=send_x.at[i, :, cols],
            dst_ref=recv_x.at[i, :, cols],
            send_sem=x_sems.at[0, i, j],
            recv_sem=x_sems.at[1, i, j],
            device_id=(me_d, lax.rem(me_x + i, xs) * 2 + me_c),
            device_id_type=MESH,
        )

    wo_s.arrived()
    for j in range(chunks):
        for d in range(j * per_chunk, (j + 1) * per_chunk):
            weights = wo_all[d]
            for t in range(tensor):
                product = dot(attended[t * toks : (t + 1) * toks, :], weights)
                part[t % 2, t // 2, :, d * columns : (d + 1) * columns] = product.astype(BF)
        pair_copy(j).start()
    for j in range(chunks):
        cols = slice(j * chunk, (j + 1) * chunk)
        pair_copy(j).wait_recv()
        for i in range(1, xs):
            x = lax.rem(me_x + i, xs)
            send_x[i, :, cols] = (
                part[me_c, x, :, cols].astype(F32) + recv_pair[x, :, cols].astype(F32)
            ).astype(BF)
            x_copy(i, j).start()
        total[:, cols] = (
            residual[:, cols].astype(F32)
            + part[me_c, me_x, :, cols].astype(F32)
            + recv_pair[me_x, :, cols].astype(F32)
        )
    for k in range(2, lines - 1):
        down_s.step(k)
    squares = jnp.zeros((toks, 1), F32)
    for j in range(chunks):
        cols = slice(j * chunk, (j + 1) * chunk)
        mid = total[:, cols]
        for i in range(1, xs):
            x_copy(i, j).wait_recv()
            mid = mid + recv_x[i, :, cols].astype(F32)
        mid = mid.astype(BF)
        hidden_out[:, cols] = mid
        mid = mid.astype(F32)
        total[:, cols] = mid
        squares = squares + jnp.sum(mid * mid, axis=1, keepdims=True)
    scale = lax.rsqrt(squares * (1.0 / width) + 1e-6)
    normed = (total[...] * scale * gain[...]).astype(BF)

    def row_copy(i):
        return pltpu.make_async_remote_copy(
            src_ref=rows_out.at[lax.div(peers[i], SPLIT)],
            dst_ref=rows_in.at[me_t],
            send_sem=row_sems.at[0, i],
            recv_sem=row_sems.at[1, i],
            device_id=(me_d, peers[i]),
            device_id_type=MESH,
        )

    def piece_copy(i):
        return pltpu.make_async_remote_copy(
            src_ref=piece_out.at[peers[i]],
            dst_ref=piece_in.at[me_t],
            send_sem=piece_sems.at[0, i],
            recv_sem=piece_sems.at[1, i],
            device_id=(me_d, peers[i]),
            device_id_type=MESH,
        )

    def from_source(i, buf, sems):
        return pltpu.make_async_remote_copy(
            src_ref=buf.at[sources[i]],
            dst_ref=buf.at[sources[i]],
            send_sem=sems.at[0, i],
            recv_sem=sems.at[1, i],
            device_id=(me_d, sources[i]),
            device_id_type=MESH,
        )

    for e in range(flight):
        chosen = jnp.transpose(picks[e])[:MOST].astype(BF)
        rows_out[e] = dot(chosen, normed).astype(BF)
    for i in range(1, tensor):
        row_copy(i).start()
    rows_in[me_t] = rows_out[lax.div(me_t, SPLIT)]
    gu_s.arrived()
    for i in range(1, tensor):
        from_source(i, rows_in, row_sems).wait_recv()
    expert_rows = rows_in[...].reshape(tensor * MOST, width)
    gate_val = dot(expert_rows, gu_all[:, 0].reshape(width, gu_all.shape[3]))
    up_val = dot(expert_rows, gu_all[:, 1].reshape(width, gu_all.shape[3]))
    inner = (gate_val * jax.nn.sigmoid(gate_val) * up_val).astype(BF)
    down_s.arrived()
    for d in range(dp):
        product = dot(inner, down_all[d]).astype(BF)
        piece_out[:, :, d * columns : (d + 1) * columns] = product.reshape(tensor, MOST, columns)
    for i in range(1, tensor):
        piece_copy(i).start()
    piece_in[me_t] = piece_out[me_t]
    for i in range(1, tensor):
        from_source(i, piece_in, piece_sems).wait_recv()
    result = jnp.zeros((toks, width), F32)
    for e in range(flight):
        summed = piece_in[e * SPLIT].astype(F32)
        for s in range(1, SPLIT):
            summed = summed + piece_in[e * SPLIT + s].astype(F32)
        high = summed.astype(BF)
        low = (summed - high.astype(F32)).astype(BF)
        pad = jnp.zeros((toks - MOST, width), BF)
        pick = picks[e].astype(BF)
        spread = dot(pick, jnp.concatenate([high, pad], axis=0)) + dot(
            pick, jnp.concatenate([low, pad], axis=0)
        )
        result = result + mixes[e] * spread
    expert_out[...] = result.astype(BF)

    for n in range(3):
        for i in range(1, tensor):
            qkv_copy(n, i).wait_send()
    for j in range(chunks):
        pair_copy(j).wait_send()
        for i in range(1, xs):
            x_copy(i, j).wait_send()
    for i in range(1, tensor):
        row_copy(i).wait_send()
        piece_copy(i).wait_send()
    for stream in streams:
        stream.sent()


def body(dp, tensor, *arrays):
    (
        residual,
        queries,
        new_keys,
        new_values,
        lengths,
        page_order,
        wo,
        gain,
        gate,
        up,
        down,
        routes,
        route_weights,
    ) = arrays
    toks, width = queries.shape
    head_width = width // tensor
    group = toks * tensor
    lines = dp // 2
    pair_stride, line_stride = (1, 2) if lines <= 4 else (lines, 1)
    rows, columns = wo.shape
    piece = gate.shape[2]
    pool = page_order.shape[1]
    flight = tensor // SPLIT
    xs = tensor // 2
    smem = pl.BlockSpec(memory_space=pltpu.SMEM)
    vmem = pl.BlockSpec(memory_space=pltpu.VMEM)
    anywhere = pl.BlockSpec(memory_space=pl.ANY)
    dma = pltpu.SemaphoreType.DMA
    return pl.pallas_call(
        functools.partial(layer_kernel, (dp, tensor, pair_stride, line_stride)),
        out_shape=(
            jax.ShapeDtypeStruct((toks, width), BF),
            jax.ShapeDtypeStruct((toks, width), BF),
            jax.ShapeDtypeStruct((pool, PAGE, head_width), BF),
            jax.ShapeDtypeStruct((pool, PAGE, head_width), BF),
        ),
        in_specs=[smem, smem] + [anywhere] * 3 + [vmem] * 8,
        out_specs=(vmem,) * 4,
        scratch_shapes=[
            pltpu.VMEM((dp, rows, columns), BF),
            pltpu.VMEM((dp, 2, columns, piece), BF),
            pltpu.VMEM((dp, piece, columns), BF),
            pltpu.VMEM((group, head_width), BF),
            pltpu.VMEM((group, head_width), BF),
            pltpu.VMEM((group, head_width), BF),
            pltpu.VMEM((group, head_width), BF),
            pltpu.VMEM((2, xs, toks, width), BF),
            pltpu.VMEM((xs, toks, width), BF),
            pltpu.VMEM((xs, toks, width), BF),
            pltpu.VMEM((xs, toks, width), BF),
            pltpu.VMEM((toks, width), F32),
            pltpu.VMEM((flight, MOST, width), BF),
            pltpu.VMEM((tensor, MOST, width), BF),
            pltpu.VMEM((tensor, MOST, width), BF),
            pltpu.VMEM((tensor, MOST, width), BF),
            dma((3, 3, 2, lines)),
            dma((3, 2, tensor)),
            dma((3,)),
            dma((2, 4)),
            dma((2, xs, 4)),
            dma((2, tensor)),
            dma((2, tensor)),
        ],
        compiler_params=pltpu.CompilerParams(
            collective_id=0, has_side_effects=True, vmem_limit_bytes=56 * 1024 * 1024
        ),
    )(
        lengths,
        page_order,
        queries,
        new_keys,
        new_values,
        residual,
        wo,
        gain.reshape(1, -1),
        gate,
        up,
        down,
        routes,
        route_weights,
    )


def solution(mesh):
    return jax.shard_map(
        functools.partial(body, mesh.shape["dp"], mesh.shape["tensor"]),
        mesh=mesh,
        in_specs=(
            P(("dp", "tensor"), None),
            P(("dp", "tensor"), None),
            P(("dp", "tensor"), None),
            P(("dp", "tensor"), None),
            P("dp", None),
            P("dp", None),
            P("tensor", "dp"),
            P(),
            P("tensor", "dp", None),
            P("tensor", "dp", None),
            P("tensor", None, "dp"),
            P(("dp", "tensor"), None),
            P(("dp", "tensor"), None),
        ),
        out_specs=(
            P(("dp", "tensor"), None),
            P(("dp", "tensor"), None),
            P("dp", None, "tensor"),
            P("dp", None, "tensor"),
        ),
        check_vma=False,
    )
```

```python
import functools
import math

import jax
import jax.numpy as jnp
from jax import lax
from jax.experimental import pallas as pl
from jax.experimental.pallas import tpu as pltpu
from jax.sharding import PartitionSpec as P

HEADS = 16
HD = 128
SPLIT = 4
PAGE = 128
MOST = 16
MESH = pl.DeviceIdType.MESH
BF = jnp.bfloat16
F32 = jnp.float32


def dot(a, b):
    return jnp.dot(a, b, preferred_element_type=F32)


class Stream:
    def __init__(self, buf, sems, place, lines, pair_stride, line_stride, me_t, chain, cross, within):
        self.buf, self.sems, self.lines, self.me_t = buf, sems, lines, me_t
        self.pos, self.side = place
        self.chain, self.cross, self.within = chain, cross, within
        self.pair_stride, self.line_stride = pair_stride, line_stride

    def shard(self, pos, side):
        return pos * self.line_stride + side * self.pair_stride

    def copy(self, kind, k, d, target):
        block = self.buf.at[(d, *self.within)]
        return pltpu.make_async_remote_copy(
            src_ref=block,
            dst_ref=block,
            send_sem=self.sems.at[kind, 0, k],
            recv_sem=self.sems.at[kind, 1, k],
            device_id=(target, self.me_t),
            device_id_type=MESH,
        )

    def up(self, k):
        return self.copy(0, k, self.shard(self.pos - k, self.chain), self.shard(self.pos + 1, self.side))

    def down(self, k):
        return self.copy(1, k, self.shard(self.pos + k, self.chain), self.shard(self.pos - 1, self.side))

    def across(self, q):
        return self.copy(2, q, self.shard(q, self.side), self.shard(self.pos, 1 - self.side))

    def start(self):
        pos, last = self.pos, self.lines - 1

        @pl.when(pos < last)
        def _():
            self.up(0).start()

        @pl.when(pos > 0)
        def _():
            self.down(0).start()

        if self.cross != 0:
            self.across(pos).start()

    def step(self, k):
        pos, last = self.pos, self.lines - 1

        @pl.when(pos - 1 - k >= 0)
        def _():
            d = self.shard(pos - 1 - k, self.chain)
            self.copy(0, k, d, self.shard(pos, self.side)).wait_recv()
            if k + 1 <= last - 1:

                @pl.when(pos < last)
                def _():
                    self.up(k + 1).start()

            if self.cross == 2:
                self.across(pos - 1 - k).start()

        @pl.when(pos + 1 + k <= last)
        def _():
            d = self.shard(pos + 1 + k, self.chain)
            self.copy(1, k, d, self.shard(pos, self.side)).wait_recv()
            if k + 1 <= last - 1:

                @pl.when(pos > 0)
                def _():
                    self.down(k + 1).start()

            if self.cross == 2:
                self.across(pos + 1 + k).start()

    def arrived(self):
        for q in range(self.lines) if self.cross == 2 else [self.pos]:
            d = self.shard(q, 1 - self.side)
            self.copy(2, q, d, self.shard(self.pos, 1 - self.side)).wait_recv()

    def sent(self):
        pos, last = self.pos, self.lines - 1
        for k in range(last):

            @pl.when((pos - k >= 0) & (pos < last))
            def _():
                self.up(k).wait_send()

            @pl.when((pos + k <= last) & (pos > 0))
            def _():
                self.down(k).wait_send()

        for q in ((), (pos,), range(self.lines))[self.cross]:
            self.across(q).wait_send()


class Streams:
    def __init__(self, members):
        self.members = members

    def start(self):
        for stream in self.members:
            stream.start()

    def step(self, k):
        for stream in self.members:
            stream.step(k)

    def arrived(self):
        for stream in self.members:
            stream.arrived()


def layer_kernel(
    dims,
    lengths,
    order,
    q_in,
    k_in,
    v_in,
    residual,
    wo,
    gain,
    gate,
    up,
    down,
    routes,
    route_weights,
    hidden_out,
    expert_out,
    key_out,
    value_out,
    wo_all,
    gu_all,
    down_all,
    q_all,
    k_all,
    v_all,
    attended,
    part,
    recv_pair,
    send_x,
    recv_x,
    total,
    rows_out,
    rows_in,
    piece_out,
    piece_in,
    weight_sems,
    qkv_sems,
    own_sems,
    pair_sems,
    x_sems,
    row_sems,
    piece_sems,
):
    dp, tensor, pair_stride, line_stride = dims
    lines = dp // 2
    toks, width = q_in.shape
    head_width = width // tensor
    heads = head_width // HD
    group = toks * tensor
    columns = wo.shape[1]
    flight = tensor // SPLIT
    xs = tensor // 2
    me_d, me_t = lax.axis_index("dp"), lax.axis_index("tensor")
    me_x, me_c = lax.div(me_t, 2), lax.rem(me_t, 2)
    if pair_stride == 1:
        pos, side = lax.div(me_d, 2), lax.rem(me_d, 2)
    else:
        pos, side = lax.rem(me_d, lines), lax.div(me_d, lines)
    place = (pos, side)
    half = wo.shape[0] // 2
    streams = [
        Stream(buf, weight_sems.at[i], place, lines, pair_stride, line_stride, me_t, chain, cross, within)
        for i, (buf, chain, cross, within) in enumerate(
            (
                (wo_all, side, 2, (pl.ds(0, half),)),
                (wo_all, side, 2, (pl.ds(half, half),)),
                (gu_all, side, 2, (0,)),
                (gu_all, side, 2, (1,)),
                (down_all, side, 1, ()),
                (down_all, 1 - side, 0, ()),
            )
        )
    ]
    wo_s, gu_s = Streams(streams[:2]), Streams(streams[2:4])
    down_s, other_s = streams[4:]
    wo_first = streams[0]
    peers = [lax.rem(me_t + i, tensor) for i in range(tensor)]
    sources = [lax.rem(me_t + tensor - i, tensor) for i in range(tensor)]

    barrier = pltpu.get_barrier_semaphore()
    for i in range(1, tensor):
        pl.semaphore_signal(barrier, inc=1, device_id=(me_d, peers[i]), device_id_type=MESH)
    pl.semaphore_signal(
        barrier, inc=1, device_id=(wo_first.shard(pos, 1 - side), me_t), device_id_type=MESH
    )

    @pl.when(pos < lines - 1)
    def _():
        pl.semaphore_signal(
            barrier, inc=1, device_id=(wo_first.shard(pos + 1, side), me_t), device_id_type=MESH
        )

    @pl.when(pos > 0)
    def _():
        pl.semaphore_signal(
            barrier, inc=1, device_id=(wo_first.shard(pos - 1, side), me_t), device_id_type=MESH
        )

    wo_all[me_d] = wo[...].astype(BF)
    neighbours = (pos < lines - 1).astype(jnp.int32) + (pos > 0).astype(jnp.int32)
    pl.semaphore_wait(barrier, tensor + neighbours)

    wo_s.start()

    mine = pl.ds(pl.multiple_of(me_t * toks, toks), toks)

    def head_cols(t):
        return pl.ds(pl.multiple_of(t * head_width, head_width), head_width)

    triples = ((q_in, q_all), (k_in, k_all), (v_in, v_all))

    def qkv_copy(n, i):
        src, dst = triples[n]
        return pltpu.make_async_remote_copy(
            src_ref=src.at[:, head_cols(peers[i])],
            dst_ref=dst.at[mine, :],
            send_sem=qkv_sems.at[n, 0, i],
            recv_sem=qkv_sems.at[n, 1, i],
            device_id=(me_d, peers[i]),
            device_id_type=MESH,
        )

    def own_copy(n):
        src, dst = triples[n]
        return pltpu.make_async_copy(src.at[:, head_cols(me_t)], dst.at[mine, :], own_sems.at[n])

    for n in range(3):
        for i in range(1, tensor):
            qkv_copy(n, i).start()
        own_copy(n).start()

    gu_all[me_d, 0] = gate[0].astype(BF)
    gu_all[me_d, 1] = up[0].astype(BF)
    down_all[me_d] = down[0].astype(BF)
    gu_s.start()
    down_s.start()

    prompts, pool = lengths.shape[1], order.shape[1]
    starts, ends, firsts = [], [], []
    begin, page = 0, 0
    for r in range(prompts):
        starts.append(begin)
        firsts.append(page)
        begin = begin + lengths[0, r]
        page = page + ((lengths[0, r] + (PAGE - 1)) >> 7)
        ends.append(begin)

    def segment_of(index):
        return sum((index >= end).astype(jnp.int32) for end in ends)

    row_index = lax.broadcasted_iota(jnp.int32, (1, group), 1)
    seg_row = segment_of(row_index)
    slot = jnp.zeros((1, group), jnp.int32)
    for r in range(prompts):
        position = row_index - starts[r]
        logical = firsts[r] + (position >> 7)
        physical = jnp.zeros((1, group), jnp.int32)
        for p in range(pool):
            physical = physical + jnp.where(logical == p, order[0, p], 0)
        slot = jnp.where(seg_row == r, physical * PAGE + (position & (PAGE - 1)), slot)

    def source_rows(i):
        return pl.ds(pl.multiple_of(sources[i] * toks, toks), toks)

    def qkv_arrived(n):
        src, dst = triples[n]
        for i in range(1, tensor):
            pltpu.make_async_remote_copy(
                src_ref=src.at[:, head_cols(me_t)],
                dst_ref=dst.at[source_rows(i), :],
                send_sem=qkv_sems.at[n, 0, i],
                recv_sem=qkv_sems.at[n, 1, i],
                device_id=(me_d, sources[i]),
                device_id_type=MESH,
            ).wait_recv()
        own_copy(n).wait()

    q_rows = min(512, group)

    def attend(h):
        cols = slice(h * HD, (h + 1) * HD)

        def block(first):
            q = q_all[pl.ds(first, q_rows), cols]
            scores = lax.dot_general(
                q, k_all[:, cols], (((1,), (1,)), ((), ())), preferred_element_type=F32
            ) * (1.0 / math.sqrt(HD))
            index = lax.broadcasted_iota(jnp.int32, (q_rows, 1), 0) + first
            scores = jnp.where(segment_of(index) == seg_row, scores, -jnp.inf)
            weights = jnp.exp(scores - jnp.max(scores, axis=1, keepdims=True))
            sums = jnp.sum(weights, axis=1, keepdims=True)
            out = dot(weights.astype(BF), v_all[:, cols]) / sums
            attended[pl.ds(first, q_rows), cols] = out.astype(BF)

        if group == q_rows:
            block(0)
        else:

            @pl.loop(0, group // q_rows)
            def _(b):
                block(pl.multiple_of(b * q_rows, q_rows))

    def write_pages(values, out):
        @pl.loop(0, pool)
        def _(p):
            wanted = lax.broadcasted_iota(jnp.int32, (PAGE, group), 0) + p * PAGE
            hit = jnp.where(wanted == slot, 1.0, 0.0).astype(BF)
            out[p] = dot(hit, values[...]).astype(BF)

    for k in range(lines - 1):
        wo_s.step(k)
    for n in range(3):
        qkv_arrived(n)
    for h in range(heads):
        attend(h)
        if h == heads // 2:
            gu_s.step(0)
    down_s.arrived()
    other_s.start()
    ids = lax.broadcasted_iota(jnp.int32, (toks, toks), 0)
    lanes = lax.broadcasted_iota(jnp.int32, (toks, toks), 1)
    upper = jnp.where(ids <= lanes, 1.0, 0.0).astype(BF)
    picks, mixes, chosen = [], [], []
    for e in range(flight):
        named = routes[...] == e
        routed = jnp.max(jnp.where(named, 1.0, 0.0), axis=0, keepdims=True)
        amount = jnp.sum(jnp.where(named, route_weights[...], 0.0), axis=0, keepdims=True)
        spread = jnp.broadcast_to(routed, (toks, toks))
        rank = dot(spread.astype(BF), upper).astype(jnp.int32) - 1
        pick = jnp.where((rank == ids) & (spread > 0.5), 1.0, 0.0)
        chosen.append(pick[:MOST].astype(BF))
        picks.append(jnp.transpose(pick).astype(BF))
        mixes.append(jnp.sum(jnp.transpose(pick * amount), axis=1, keepdims=True))

    chunks = 4
    chunk = width // chunks
    per_chunk = dp // chunks
    partner = (me_d, me_t + 1 - 2 * me_c)

    def pair_copy(j):
        cols = pl.ds(j * chunk, chunk)
        return pltpu.make_async_remote_copy(
            src_ref=part.at[1 - me_c, :, :, cols],
            dst_ref=recv_pair.at[:, :, cols],
            send_sem=pair_sems.at[0, j],
            recv_sem=pair_sems.at[1, j],
            device_id=partner,
            device_id_type=MESH,
        )

    def x_copy(i, j):
        cols = pl.ds(j * chunk, chunk)
        return pltpu.make_async_remote_copy(
            src_ref=send_x.at[i, :, cols],
            dst_ref=recv_x.at[i, :, cols],
            send_sem=x_sems.at[0, i, j],
            recv_sem=x_sems.at[1, i, j],
            device_id=(me_d, lax.rem(me_x + i, xs) * 2 + me_c),
            device_id_type=MESH,
        )

    wo_s.arrived()
    for j in range(chunks):
        for d in range(j * per_chunk, (j + 1) * per_chunk):
            weights = wo_all[d]
            for t in range(tensor):
                product = dot(attended[t * toks : (t + 1) * toks, :], weights)
                part[t % 2, t // 2, :, d * columns : (d + 1) * columns] = product.astype(BF)
        pair_copy(j).start()
    gu_s.step(1)
    for j in range(chunks):
        cols = slice(j * chunk, (j + 1) * chunk)
        pair_copy(j).wait_recv()
        for i in range(1, xs):
            x = lax.rem(me_x + i, xs)
            send_x[i, :, cols] = (
                part[me_c, x, :, cols].astype(F32) + recv_pair[x, :, cols].astype(F32)
            ).astype(BF)
            x_copy(i, j).start()
        total[:, cols] = (
            residual[:, cols].astype(F32)
            + part[me_c, me_x, :, cols].astype(F32)
            + recv_pair[me_x, :, cols].astype(F32)
        )
    write_pages(k_all, key_out)
    down_s.step(0)
    other_s.step(0)
    for k in range(2, lines - 1):
        gu_s.step(k)
        down_s.step(k - 1)
        other_s.step(k - 1)
    write_pages(v_all, value_out)
    down_s.step(lines - 2)
    other_s.step(lines - 2)
    squares = jnp.zeros((toks, 1), F32)
    for j in range(chunks):
        cols = slice(j * chunk, (j + 1) * chunk)
        mid = total[:, cols]
        for i in range(1, xs):
            x_copy(i, j).wait_recv()
            mid = mid + recv_x[i, :, cols].astype(F32)
        mid = mid.astype(BF)
        hidden_out[:, cols] = mid
        mid = mid.astype(F32)
        total[:, cols] = mid
        squares = squares + jnp.sum(mid * mid, axis=1, keepdims=True)
    scale = lax.rsqrt(squares * (1.0 / width) + 1e-6)
    normed = (total[...] * scale * gain[...]).astype(BF)

    def row_copy(i):
        return pltpu.make_async_remote_copy(
            src_ref=rows_out.at[lax.div(peers[i], SPLIT)],
            dst_ref=rows_in.at[me_t],
            send_sem=row_sems.at[0, i],
            recv_sem=row_sems.at[1, i],
            device_id=(me_d, peers[i]),
            device_id_type=MESH,
        )

    def piece_copy(i):
        return pltpu.make_async_remote_copy(
            src_ref=piece_out.at[peers[i]],
            dst_ref=piece_in.at[me_t],
            send_sem=piece_sems.at[0, i],
            recv_sem=piece_sems.at[1, i],
            device_id=(me_d, peers[i]),
            device_id_type=MESH,
        )

    def from_source(i, buf, sems):
        return pltpu.make_async_remote_copy(
            src_ref=buf.at[sources[i]],
            dst_ref=buf.at[sources[i]],
            send_sem=sems.at[0, i],
            recv_sem=sems.at[1, i],
            device_id=(me_d, sources[i]),
            device_id_type=MESH,
        )

    for e in range(flight):
        rows_out[e] = dot(chosen[e], normed).astype(BF)
    for i in range(1, tensor):
        row_copy(i).start()
    rows_in[me_t] = rows_out[lax.div(me_t, SPLIT)]
    gu_s.arrived()
    for i in range(1, tensor):
        from_source(i, rows_in, row_sems).wait_recv()
    expert_rows = rows_in[...].reshape(tensor * MOST, width)
    gate_val = dot(expert_rows, gu_all[:, 0].reshape(width, gu_all.shape[3]))
    up_val = dot(expert_rows, gu_all[:, 1].reshape(width, gu_all.shape[3]))
    inner = (gate_val * jax.nn.sigmoid(gate_val) * up_val).astype(BF)
    for d in range(dp):
        product = dot(inner, down_all[d]).astype(BF)
        piece_out[:, :, d * columns : (d + 1) * columns] = product.reshape(tensor, MOST, columns)
    for i in range(1, tensor):
        piece_copy(i).start()
    piece_in[me_t] = piece_out[me_t]
    for i in range(1, tensor):
        from_source(i, piece_in, piece_sems).wait_recv()
    result = jnp.zeros((toks, width), F32)
    for e in range(flight):
        summed = piece_in[e * SPLIT].astype(F32)
        for s in range(1, SPLIT):
            summed = summed + piece_in[e * SPLIT + s].astype(F32)
        high = summed.astype(BF)
        low = (summed - high.astype(F32)).astype(BF)
        pad = jnp.zeros((toks - MOST, width), BF)
        pick = picks[e]
        spread = dot(pick, jnp.concatenate([high, pad], axis=0)) + dot(
            pick, jnp.concatenate([low, pad], axis=0)
        )
        result = result + mixes[e] * spread
    expert_out[...] = result.astype(BF)

    for n in range(3):
        for i in range(1, tensor):
            qkv_copy(n, i).wait_send()
    for j in range(chunks):
        pair_copy(j).wait_send()
        for i in range(1, xs):
            x_copy(i, j).wait_send()
    for i in range(1, tensor):
        row_copy(i).wait_send()
        piece_copy(i).wait_send()
    for stream in streams:
        stream.sent()


def body(dp, tensor, *arrays):
    (
        residual,
        queries,
        new_keys,
        new_values,
        lengths,
        page_order,
        wo,
        gain,
        gate,
        up,
        down,
        routes,
        route_weights,
    ) = arrays
    toks, width = queries.shape
    head_width = width // tensor
    group = toks * tensor
    lines = dp // 2
    pair_stride, line_stride = (1, 2) if lines <= 4 else (lines, 1)
    rows, columns = wo.shape
    piece = gate.shape[2]
    pool = page_order.shape[1]
    flight = tensor // SPLIT
    xs = tensor // 2
    smem = pl.BlockSpec(memory_space=pltpu.SMEM)
    vmem = pl.BlockSpec(memory_space=pltpu.VMEM)
    anywhere = pl.BlockSpec(memory_space=pl.ANY)
    dma = pltpu.SemaphoreType.DMA
    return pl.pallas_call(
        functools.partial(layer_kernel, (dp, tensor, pair_stride, line_stride)),
        out_shape=(
            jax.ShapeDtypeStruct((toks, width), BF),
            jax.ShapeDtypeStruct((toks, width), BF),
            jax.ShapeDtypeStruct((pool, PAGE, head_width), BF),
            jax.ShapeDtypeStruct((pool, PAGE, head_width), BF),
        ),
        in_specs=[smem, smem] + [anywhere] * 3 + [vmem] * 8,
        out_specs=(vmem,) * 4,
        scratch_shapes=[
            pltpu.VMEM((dp, rows, columns), BF),
            pltpu.VMEM((dp, 2, columns, piece), BF),
            pltpu.VMEM((dp, piece, columns), BF),
            pltpu.VMEM((group, head_width), BF),
            pltpu.VMEM((group, head_width), BF),
            pltpu.VMEM((group, head_width), BF),
            pltpu.VMEM((group, head_width), BF),
            pltpu.VMEM((2, xs, toks, width), BF),
            pltpu.VMEM((xs, toks, width), BF),
            pltpu.VMEM((xs, toks, width), BF),
            pltpu.VMEM((xs, toks, width), BF),
            pltpu.VMEM((toks, width), F32),
            pltpu.VMEM((flight, MOST, width), BF),
            pltpu.VMEM((tensor, MOST, width), BF),
            pltpu.VMEM((tensor, MOST, width), BF),
            pltpu.VMEM((tensor, MOST, width), BF),
            dma((6, 3, 2, lines)),
            dma((3, 2, tensor)),
            dma((3,)),
            dma((2, 4)),
            dma((2, xs, 4)),
            dma((2, tensor)),
            dma((2, tensor)),
        ],
        compiler_params=pltpu.CompilerParams(
            collective_id=0, has_side_effects=True, vmem_limit_bytes=56 * 1024 * 1024
        ),
    )(
        lengths,
        page_order,
        queries,
        new_keys,
        new_values,
        residual,
        wo,
        gain.reshape(1, -1),
        gate,
        up,
        down,
        routes.T,
        route_weights.T,
    )


def solution(mesh):
    return jax.shard_map(
        functools.partial(body, mesh.shape["dp"], mesh.shape["tensor"]),
        mesh=mesh,
        in_specs=(
            P(("dp", "tensor"), None),
            P(("dp", "tensor"), None),
            P(("dp", "tensor"), None),
            P(("dp", "tensor"), None),
            P("dp", None),
            P("dp", None),
            P("tensor", "dp"),
            P(),
            P("tensor", "dp", None),
            P("tensor", "dp", None),
            P("tensor", None, "dp"),
            P(("dp", "tensor"), None),
            P(("dp", "tensor"), None),
        ),
        out_specs=(
            P(("dp", "tensor"), None),
            P(("dp", "tensor"), None),
            P("dp", None, "tensor"),
            P("dp", None, "tensor"),
        ),
        check_vma=False,
    )
```
